128 devices in a mesh: section: 32 (over y, x, core), expert: 4 (over z).
Axes of the slice: x: 4, y: 4, z: 4, core: 2. Of those that a mesh axis runs over, the one named last changes fastest.
Arguments:
- x_a: bfloat16 [2048, 4096], P('section', 'expert'), may hold values from -6 to 6
- ids_a: int32 [2048, 8], P('section'), may hold values from 0 to 31, all different within a row; in each aligned block of 64 rows (0 to 63, 64 to 127, ...) at most 20 rows name the same one
- prob_a: float32 [2048, 8], P('section'), may hold values from 0.05 to 0.5
- x_b: bfloat16 [2048, 4096], P('section', 'expert'), may hold values from -6 to 6
- ids_b: int32 [2048, 8], P('section'), may hold values from 0 to 31, all different within a row; in each aligned block of 64 rows (0 to 63, 64 to 127, ...) at most 20 rows name the same one
- prob_b: float32 [2048, 8], P('section'), may hold values from 0.05 to 0.5
- cot_b: bfloat16 [2048, 4096], P('section', 'expert'), may hold values from -6 to 6
- w_gate: bfloat16 [32, 4096, 2048], P('section', None, 'expert'), may hold values from -0.09375 to 0.09375
- w_up: bfloat16 [32, 4096, 2048], P('section', None, 'expert'), may hold values from -0.09375 to 0.09375
- w_down: bfloat16 [32, 2048, 4096], P('section', 'expert'), may hold values from -0.125 to 0.125
Outputs:
- out_a: bfloat16 [2048, 4096], P('section', 'expert')
- grad_b: bfloat16 [2048, 4096], P('section', 'expert')
The draws below stay inside these ranges and needn't reach their ends.
Inputs may be any that keep to these rules, and one draw needn't show every extreme that they name: `ids_a`: each row names 8 different experts. In each aligned block of 64 rows no expert is named more than 20 times, a bound that some block reaches. `ids_b`: as for ids_a.
All inputs are finite; a program needn't handle non-finite values.
Results may differ from the reference program's by a relative error of at most 0.017.
Values may be sent and summed in bfloat16 or wider, within the bound.
No kernel may reach another device: no remote copies, remote signals or barrier semaphores. Data moves between devices by JAX's collectives and lax.ppermute only.
A program may use at most 128 MiB of HBM per device.

```python
import math
import jax
import jax.numpy as jnp
import numpy as np
from jax import lax

D = 4096
FF = 2048
TOPK = 8
TOK_DEV = 64
EXPERTS = 32
CAP = 20
TOKENS = 2048
N_SECTION = 32
N_EXPERT = 4


def block_levels(rng, shape, pieces, smallest, top_value):
    loudness, own = 1.0, jax.random.fold_in(rng, 6)
    for dim, blocks in pieces:
        steps = jnp.exp(jax.random.uniform(jax.random.fold_in(own, dim), (blocks,), jnp.float32, smallest / len(pieces), top_value / len(pieces)))
        loudness = loudness * jnp.repeat(steps, shape[dim] // blocks).reshape([-1 if axis == dim else 1 for axis in range(len(shape))])
    return loudness


def routed_block(rng, own, number, rows, number_of, top, reach, slope):
    sequence = jax.random.permutation(rng, number_of)
    crowded, common = shares(number_of, rows * top, reach, slope, True), shares(number_of, rows * top, reach, slope, False)
    places = jnp.arange(number_of)

    def named(tallies, offset_by):
        used = int((tallies > 0).sum())
        fixed = max(1, used // 4)
        passed = fixed + (places - fixed + offset_by * (used - fixed)) % max(1, number_of - fixed)
        return jnp.zeros((number_of,), jnp.int32).at[sequence[jnp.where(places < fixed, places, passed)]].set(jnp.asarray(tallies, jnp.int32))

    tallies = jnp.where(number % 4 == 0, named(crowded, number // 4), named(common, number - number // 4 - 1))
    mixed = jax.random.permutation(jax.random.fold_in(own, 3), number_of)
    giver, receiver = mixed[0:number_of // 2 * 2:2], mixed[1:number_of // 2 * 2:2]
    slack = jnp.minimum(tallies[giver] - 1, reach - tallies[receiver]) // 2
    slack = jnp.where((giver == sequence[0]) | (receiver == sequence[0]) | (tallies[receiver] == 0), 0, jnp.maximum(slack, 0))
    passed = jax.random.randint(jax.random.fold_in(own, 4), (number_of // 2,), 0, 1 << 20) % (slack + 1)
    tallies = tallies.at[giver].add(-passed).at[receiver].add(passed)
    items = jnp.searchsorted(jnp.cumsum(tallies), jnp.arange(rows * top), side="right").astype(jnp.int32)
    listing = items.reshape(top, rows).T
    listing = listing[jax.random.permutation(jax.random.fold_in(own, 1), rows)]
    offset_by = jax.random.randint(jax.random.fold_in(own, 2), (rows, 1), 0, top)
    return jnp.take_along_axis(listing, (jnp.arange(top)[None, :] + offset_by) % top, axis=1)


def shares(number_of, total, limit, lean, full):
    weights = [(1 << 20) // math.isqrt(standing ** lean) + 1 for standing in range(1, number_of + 1)]
    largest = limit if full else min(limit, max(-(-total // number_of), total * weights[0] // sum(weights)))
    least = 1 if total - largest >= number_of - 1 else 0
    given, rest = [largest] + [least] * (number_of - 1), total - largest - least * (number_of - 1)
    while rest > 0:
        movable = [i for i in range(1, number_of) if given[i] < largest] or [i for i in range(1, number_of) if given[i] < limit]
        whole, left = sum([weights[i] for i in movable]), rest
        for i in movable:
            more = min(limit - given[i], max(1, left * weights[i] // whole), rest)
            given[i] = given[i] + more
            rest = rest - more
    return np.array(given)


def noise(own_key, shape, width, bound, shards=(), held_as=jnp.bfloat16):
    values = jax.random.normal(own_key, shape, jnp.float32) * width
    if len(shards) > 0:
        values = block_levels(own_key, shape, shards, -0.22, 0.18) * values
    return jnp.clip(values, min=-bound, max=bound).astype(held_as)


def setup_inputs(seed: int = 0) -> dict:
    key_list = jax.random.split(jax.random.key(seed), 11)
    x_a = noise(key_list[0], (TOKENS, D), 1.0, 6.0, ((0, 32), (1, 4)))
    ids_a_keys = jax.random.split(jax.random.fold_in(key_list[1], 1), TOKENS // TOK_DEV)
    ids_a_turns = jax.random.permutation(jax.random.fold_in(key_list[1], 3), TOKENS // TOK_DEV)
    ids_a = jax.vmap(lambda own, number: routed_block(jax.random.fold_in(key_list[1], 2), own, number, TOK_DEV, EXPERTS, TOPK, CAP, 1))(ids_a_keys, ids_a_turns).reshape((TOKENS, TOPK))
    prob_a = jnp.clip(jnp.exp(math.log(0.5) - 2.3025851 * jax.random.uniform(key_list[2], (TOKENS, TOPK), jnp.float32) ** block_levels(key_list[2], (TOKENS, TOPK), ((0, 32),), -0.2, 0.2)), 0.05, 0.5)
    x_b = noise(key_list[3], (TOKENS, D), 1.0, 6.0, ((0, 32), (1, 4)))
    ids_b_keys = jax.random.split(jax.random.fold_in(key_list[4], 1), TOKENS // TOK_DEV)
    ids_b_turns = jax.random.permutation(jax.random.fold_in(key_list[4], 3), TOKENS // TOK_DEV)
    ids_b = jax.vmap(lambda own, number: routed_block(jax.random.fold_in(key_list[4], 2), own, number, TOK_DEV, EXPERTS, TOPK, CAP, 1))(ids_b_keys, ids_b_turns).reshape((TOKENS, TOPK))
    prob_b = jnp.clip(jnp.exp(math.log(0.5) - 2.3025851 * jax.random.uniform(key_list[5], (TOKENS, TOPK), jnp.float32) ** block_levels(key_list[5], (TOKENS, TOPK), ((0, 32),), -0.2, 0.2)), 0.05, 0.5)
    cot_b = noise(key_list[6], (TOKENS, D), 1.0, 6.0, ((0, 32), (1, 4)))
    w_gate = noise(key_list[7], (EXPERTS, D, FF), D ** -0.5, 0.09375, ((0, 32), (2, 4)))
    w_up = noise(key_list[8], (EXPERTS, D, FF), D ** -0.5, 0.09375, ((0, 32), (2, 4)))
    w_down = noise(key_list[9], (EXPERTS, FF, D), FF ** -0.5, 0.125, ((0, 32), (1, 4)))
    return {"x_a": x_a, "ids_a": ids_a, "prob_a": prob_a, "x_b": x_b, "ids_b": ids_b, "prob_b": prob_b, "cot_b": cot_b, "w_gate": w_gate, "w_up": w_up, "w_down": w_down}


def expert_forward(inputs, gate_cols, up_cols, down_rows):
    group_width = FF // N_EXPERT
    summed = jnp.zeros((inputs.shape[0], D), jnp.float32)
    for group_index in range(N_EXPERT):
        start = group_index * group_width
        gate_out = jnp.dot(inputs, gate_cols[:, start:start + group_width], preferred_element_type=jnp.float32)
        upward = jnp.dot(inputs, up_cols[:, start:start + group_width], preferred_element_type=jnp.float32)
        hidden = (jax.nn.silu(gate_out) * upward).astype(jnp.bfloat16)
        partial_value = jnp.dot(hidden, down_rows[start:start + group_width], preferred_element_type=jnp.float32)
        summed = summed + partial_value.astype(jnp.bfloat16).astype(jnp.float32)
    return summed.astype(jnp.bfloat16)


def expert_backward(inputs, cotangent, gate_cols, up_cols, down_rows):
    group_width = FF // N_EXPERT
    contract = (((1,), (1,)), ((), ()))
    summed = jnp.zeros((inputs.shape[0], D), jnp.float32)
    for group_index in range(N_EXPERT):
        start = group_index * group_width
        gate_slice = gate_cols[:, start:start + group_width]
        up_slice = up_cols[:, start:start + group_width]
        gate_out = jnp.dot(inputs, gate_slice, preferred_element_type=jnp.float32)
        upward = jnp.dot(inputs, up_slice, preferred_element_type=jnp.float32)
        sigmoid_gate = jax.nn.sigmoid(gate_out)
        hidden_grad = lax.dot_general(cotangent, down_rows[start:start + group_width], contract, preferred_element_type=jnp.float32)
        gate_grad = (hidden_grad * upward * sigmoid_gate * (1.0 + gate_out * (1.0 - sigmoid_gate))).astype(jnp.bfloat16)
        up_grad = (hidden_grad * gate_out * sigmoid_gate).astype(jnp.bfloat16)
        partial_value = lax.dot_general(gate_grad, gate_slice, contract, preferred_element_type=jnp.float32)
        partial_value = partial_value + lax.dot_general(up_grad, up_slice, contract, preferred_element_type=jnp.float32)
        summed = summed + partial_value.astype(jnp.bfloat16).astype(jnp.float32)
    return summed.astype(jnp.bfloat16)


def reference(x_a, ids_a, prob_a, x_b, ids_b, prob_b, cot_b, w_gate, w_up, w_down):
    slot_limit = N_SECTION * CAP

    def select_routes(idents, route_probs, expert):
        matches = idents == expert
        weight = jnp.sum(jnp.where(matches, route_probs, 0.0), axis=1)
        chosen = jnp.any(matches, axis=1)
        token_order = jnp.argsort(jnp.where(chosen, 0, 1).astype(jnp.int32), stable=True)[:slot_limit].astype(jnp.int32)
        route_scale = jnp.where(chosen[token_order], weight[token_order], 0.0)
        return token_order, route_scale

    def expert_step(totals, stacked):
        gate_cols, up_cols, down_rows, expert = stacked
        forward_sum, backward_sum = totals
        token_order, route_scale = select_routes(ids_a, prob_a, expert)
        outputs = expert_forward(x_a[token_order], gate_cols, up_cols, down_rows)
        forward_sum = forward_sum.at[token_order].add(route_scale[:, None] * outputs.astype(jnp.float32))
        token_order, route_scale = select_routes(ids_b, prob_b, expert)
        grads = expert_backward(x_b[token_order], cot_b[token_order], gate_cols, up_cols, down_rows)
        backward_sum = backward_sum.at[token_order].add(route_scale[:, None] * grads.astype(jnp.float32))
        return (forward_sum, backward_sum), None

    zeros_init = jnp.zeros((TOKENS, D), jnp.float32)
    experts_list = jnp.arange(EXPERTS, dtype=jnp.int32)
    (forward_sum, backward_sum), unused = lax.scan(expert_step, (zeros_init, zeros_init), (w_gate, w_up, w_down, experts_list))
    return forward_sum.astype(jnp.bfloat16), backward_sum.astype(jnp.bfloat16)
```

```python
import functools

import jax
import jax.numpy as jnp
from jax import lax
from jax.experimental import pallas as pl
from jax.experimental.pallas import tpu as pltpu
from jax.sharding import PartitionSpec as P

TOK = 64
CAP = 20
HALF = 512
CORES = 2
ROWS = 16 * CAP
GROUP = 4 * TOK
SLOTS = 4 * CAP
META = 128
BASES = (0, 64)
NEAR_A = 0
META_A = HALF
NEAR_B = HALF + META
META_B = 3 * HALF + META
BF16 = jnp.bfloat16
F32 = jnp.float32


def _section_moves(move):
    pairs = []
    for y in range(4):
        for x in range(4):
            for core in range(CORES):
                axis, shift = move[core]
                there_y = (y + shift) % 4 if axis == "y" else y
                there_x = (x + shift) % 4 if axis == "x" else x
                there_core = 1 - core if axis == "core" else core
                pairs.append(((y * 4 + x) * 2 + core, (there_y * 4 + there_x) * 2 + there_core))
    return pairs


def _shifts(axes):
    return [None] + [_section_moves(tuple((a, s) for a in axes)) for s in (1, 2, 3)]


def _groups(axes):
    groups = []
    for core in range(CORES):
        for other in range(4):
            if axes[core] == "y":
                groups.append([(i * 4 + other) * 2 + core for i in range(4)])
            else:
                groups.append([(other * 4 + i) * 2 + core for i in range(4)])
    return groups


FIRST = ("section", _shifts("yx"))
LAST = ("section", _shifts("xy"))
DEPTH = ("expert", [None] + [[(i, (i + s) % 4) for i in range(4)] for s in (1, 2, 3)])
LAST_GROUPS = _groups("xy")
SWAP = _section_moves((("core", 0), ("core", 0)))


def spread(values, ring):
    axis, shifts = ring
    return [values] + [lax.ppermute(values, axis, shifts[4 - d]) for d in (1, 2, 3)]


def collect(parts, ring):
    axis, shifts = ring
    arrived = [lax.ppermute(parts[d], axis, shifts[d]) for d in (1, 2, 3)]
    total = parts[0].astype(F32)
    for part in arrived:
        total = total + part.astype(F32)
    return total.astype(BF16)


def swap(values):
    return lax.ppermute(values, "section", SWAP)


def dot(a, b):
    return jnp.dot(a, b, preferred_element_type=F32)


def dot_last(a, b):
    return lax.dot_general(a, b, (((1,), (1,)), ((), ())), preferred_element_type=F32)


def dot_first(a, b):
    return lax.dot_general(a, b, (((0,), (0,)), ((), ())), preferred_element_type=F32)


def params(mib):
    return pltpu.CompilerParams(vmem_limit_bytes=mib * 2**20)


def cost(flops, moved, transcendentals=0):
    return pl.CostEstimate(flops=flops // 64, bytes_accessed=moved // 64, transcendentals=0)


def slot_matrices(meta, here, sibling):
    rows = lax.broadcasted_iota(jnp.int32, (8, META), 0)
    lanes = lax.broadcasted_iota(jnp.int32, (8, META), 1)
    expert = jnp.where(rows % 2 == 0, here, sibling)
    wanted = jnp.where(rows < 2, BASES[0] + expert, jnp.where(rows < 4, BASES[1] + expert, -1))
    select = (lanes == wanted).astype(F32).astype(BF16)
    routed = (meta.astype(F32) > 0.0).astype(F32).astype(BF16)
    match = dot_last(select, routed)
    before = lax.broadcasted_iota(jnp.int32, (GROUP, GROUP), 0)
    token = lax.broadcasted_iota(jnp.int32, (GROUP, GROUP), 1)
    same = jnp.logical_and(before < token, before // TOK == token // TOK)
    rank = dot(match.astype(BF16), same.astype(F32).astype(BF16))
    block = lax.broadcasted_iota(jnp.int32, (8, GROUP), 1) // TOK
    place = jnp.where(match > 0.5, block * CAP + rank.astype(jnp.int32), -1)
    slot = lax.broadcasted_iota(jnp.int32, (SLOTS, GROUP), 0)
    pieces = [(slot == place[i : i + 1, :]).astype(F32) for i in range(4)]
    return [jnp.concatenate(pieces[i : i + 2], axis=0).astype(BF16) for i in (0, 2)]


def gather_first_kernel(where, *refs):
    parts, (own_ref, sibling_ref, ahead_ref, back_ref) = refs[:4], refs[4:]
    for group in range(4):
        values = parts[group][...]
        meta = values[:, 3 * HALF :]
        ahead, back = slot_matrices(meta, where[1], where[2])
        ahead_ref[group] = ahead
        back_ref[group] = back
        place = slice(group * SLOTS, (group + 1) * SLOTS)
        for slots, begin, end, column in (
            (ahead, 0, HALF, NEAR_A),
            (ahead, 3 * HALF, 3 * HALF + META, META_A),
            (back, HALF, 3 * HALF, NEAR_B),
            (back, 3 * HALF, 3 * HALF + META, META_B),
        ):
            picked = dot(slots, values[:, begin:end]).astype(BF16)
            own_ref[place, column : column + end - begin] = picked[:SLOTS]
            sibling_ref[place, column : column + end - begin] = picked[SLOTS:]


def gather_first(where, parts):
    width = 3 * HALF + 2 * META
    rows = jax.ShapeDtypeStruct((ROWS, width), BF16)
    slots = jax.ShapeDtypeStruct((4, 2 * SLOTS, GROUP), BF16)
    whole = pl.BlockSpec(memory_space=pltpu.VMEM)
    return pl.pallas_call(
        gather_first_kernel,
        in_specs=[pl.BlockSpec(memory_space=pltpu.SMEM)] + [whole] * 4,
        out_specs=[whole] * 4,
        out_shape=[rows, rows, slots, slots],
        compiler_params=params(16),
        cost_estimate=cost(2 * 4 * 2 * SLOTS * GROUP * width, 6 * 2**20),
    )(where, *parts)


def along(where, distance, width):
    start = lax.rem(where[0] + distance, 4) * width
    return pl.ds(pl.multiple_of(start, HALF), HALF)


def gather_last_kernel(where, slots_ref, values_ref, own_ref, sibling_ref):
    for z in range(4):
        values = jnp.concatenate(
            [values_ref[pl.ds((4 * part + z) * TOK, TOK), :] for part in range(4)], axis=0
        )
        picked = dot(slots_ref[0], values).astype(BF16)
        columns = along(where, z, HALF)
        own_ref[:, columns] = picked[:SLOTS]
        sibling_ref[:, columns] = picked[SLOTS:]


def gather_last(where, slots, values):
    tensors = values.shape[1] // HALF
    shape = jax.ShapeDtypeStruct((ROWS, tensors * 4 * HALF), BF16)
    return pl.pallas_call(
        gather_last_kernel,
        grid_spec=pltpu.PrefetchScalarGridSpec(
            num_scalar_prefetch=1,
            grid=(tensors, 4),
            in_specs=[
                pl.BlockSpec((1, 2 * SLOTS, GROUP), lambda t, i, w: (i, 0, 0)),
                pl.BlockSpec((4 * GROUP, HALF), lambda t, i, w: (lax.rem(w[3] + i, 4), t)),
            ],
            out_specs=[pl.BlockSpec((SLOTS, 4 * HALF), lambda t, i, w: (i, t))] * 2,
        ),
        out_shape=[shape, shape],
        compiler_params=params(16),
        cost_estimate=cost(
            2 * 16 * 2 * SLOTS * GROUP * HALF * tensors, 14 * 2**20 * tensors
        ),
    )(where, slots, values)


def scatter_first_kernel(slots_ref, own_ref, sibling_ref, *outs):
    for group in range(4):
        place = slice(group * SLOTS, (group + 1) * SLOTS)
        rows = jnp.concatenate([own_ref[place, :], sibling_ref[place, :]], axis=0)
        outs[group][...] = dot_first(slots_ref[group], rows).astype(BF16)


def scatter_first(slots, own, sibling):
    whole = pl.BlockSpec(memory_space=pltpu.VMEM)
    return pl.pallas_call(
        scatter_first_kernel,
        in_specs=[whole] * 3,
        out_specs=[whole] * 4,
        out_shape=[jax.ShapeDtypeStruct((GROUP, HALF), BF16)] * 4,
        compiler_params=params(16),
        cost_estimate=cost(2 * 4 * 2 * SLOTS * GROUP * HALF, 3 * 2**20),
    )(slots, own, sibling)


def scatter_last_kernel(where, slots_ref, own_ref, sibling_ref, out_ref):
    for z in range(4):
        columns = along(where, z, HALF)
        rows = jnp.concatenate([own_ref[:, columns], sibling_ref[:, columns]], axis=0)
        dense = dot_first(slots_ref[0], rows).astype(BF16)
        for part in range(4):
            out_ref[pl.ds((4 * part + z) * TOK, TOK), :] = dense[part * TOK : (part + 1) * TOK]


def scatter_last(where, slots, own, sibling):
    return pl.pallas_call(
        scatter_last_kernel,
        grid_spec=pltpu.PrefetchScalarGridSpec(
            num_scalar_prefetch=1,
            grid=(4,),
            in_specs=[pl.BlockSpec((1, 2 * SLOTS, GROUP), lambda i, w: (i, 0, 0))]
            + [pl.BlockSpec((SLOTS, 4 * HALF), lambda i, w: (i, 0))] * 2,
            out_specs=pl.BlockSpec((4 * GROUP, HALF), lambda i, w: (lax.rem(w[3] + i, 4), 0)),
        ),
        out_shape=jax.ShapeDtypeStruct((16 * GROUP, HALF), BF16),
        compiler_params=params(16),
        cost_estimate=cost(2 * 16 * 2 * SLOTS * GROUP * HALF, 14 * 2**20),
    )(where, slots, own, sibling)


def lay_out(where, near, last, out_ref):
    for z in range(4):
        out_ref[:, along(where, z, 2 * HALF)] = near[z]
        out_ref[:, (2 * z + 1) * HALF : (2 * z + 2) * HALF] = last[z]


def halves(ref, first=0):
    return [ref[:, first + z * HALF : first + (z + 1) * HALF] for z in range(4)]


def write_result(where, weight, product, near_out, last_out):
    step = pl.program_id(0)
    for z in range(4):
        near_out[z][...] = (product(along(where, z, 2 * HALF)) * weight).astype(BF16)
    for z in range(4):
        value = (product(pl.ds((2 * z + 1) * HALF, HALF)) * weight).astype(BF16)
        for part in range(2):

            @pl.when(step == part)
            def _():
                last_out[part][:, z * HALF : (z + 1) * HALF] = value


def pick(refs):
    return jnp.where(pl.program_id(0) == 0, refs[0][...], refs[1][...])


def slot_weight(rows, base, expert):
    lanes = lax.broadcasted_iota(jnp.int32, (ROWS, META), 1)
    chosen = jnp.logical_or(lanes == base + expert, lanes == base + 32 + expert)
    return jnp.sum(jnp.where(chosen, rows.astype(F32), 0.0), axis=1, keepdims=True)


def forward_kernel(where, *refs):
    near, last, metas, (gate_ref, up_ref, down_ref) = refs[:4], refs[4:6], refs[6:8], refs[8:11]
    near_out, last_out, (values, hidden) = refs[11:15], refs[15:17], refs[17:]
    near = [r[...] for r in near]
    for part in range(2):

        @pl.when(pl.program_id(0) == part)
        def _():
            lay_out(where, near, halves(last[part]), values)

    gate = dot(values[...], gate_ref[0])
    upward = dot(values[...], up_ref[0])
    hidden[...] = (gate / (1.0 + jnp.exp(-gate)) * upward).astype(BF16)
    weight = slot_weight(pick(metas), BASES[0], where[1])

    def product(columns):
        return dot(hidden[...], down_ref[0, :, columns])

    write_result(where, weight, product, near_out, last_out)


def backward_kernel(where, *refs):
    near, last, metas, (gate_ref, up_ref, down_ref) = refs[:4], refs[4:6], refs[6:8], refs[8:11]
    near_out, last_out, (values, cotangent, gate_grad, up_grad) = refs[11:15], refs[15:17], refs[17:]
    for part in range(2):

        @pl.when(pl.program_id(0) == part)
        def _():
            lay_out(where, [r[:, :HALF] for r in near], halves(last[part]), values)
            lay_out(where, [r[:, HALF:] for r in near], halves(last[part], 4 * HALF), cotangent)

    gate = dot(values[...], gate_ref[0])
    upward = dot(values[...], up_ref[0])
    grad = dot_last(cotangent[...], down_ref[0])
    sigmoid = 1.0 / (1.0 + jnp.exp(-gate))
    scaled = grad * sigmoid
    gate_grad[...] = (scaled * upward * (1.0 + gate * (1.0 - sigmoid))).astype(BF16)
    up_grad[...] = (scaled * gate).astype(BF16)
    weight = slot_weight(pick(metas), BASES[1], where[1])

    def product(rows):
        return dot_last(gate_grad[...], gate_ref[0, rows]) + dot_last(up_grad[...], up_ref[0, rows])

    write_result(where, weight, product, near_out, last_out)


def expert_call(backward, where, near, last, rows, w_gate, w_up, w_down):
    wide = w_gate.shape[2]
    column = (META_B if backward else META_A) // META
    once = pl.Buffered(1)
    in_specs = [pl.BlockSpec((ROWS, p.shape[1]), lambda i, w: (i, 0)) for p in near]
    in_specs += [pl.BlockSpec(p.shape, lambda i, w: (0, 0), pipeline_mode=once) for p in last]
    in_specs += [
        pl.BlockSpec((ROWS, META), lambda i, w: (0, column), pipeline_mode=once) for _ in rows
    ]
    weights = [w_gate, w_up, w_down]
    in_specs += [
        pl.BlockSpec(p.shape, lambda i, w: (0, 0, 0), pipeline_mode=once) for p in weights
    ]
    out_specs = [pl.BlockSpec((ROWS, HALF), lambda i, w: (i, 0))] * 4
    out_specs += [
        pl.BlockSpec((ROWS, 4 * HALF), lambda i, w: (0, 0), pipeline_mode=once) for _ in rows
    ]
    out_shape = [jax.ShapeDtypeStruct((2 * ROWS, HALF), BF16)] * 4
    out_shape += [jax.ShapeDtypeStruct((ROWS, 4 * HALF), BF16)] * 2
    laid = pltpu.VMEM((ROWS, 8 * HALF), BF16)
    narrow = pltpu.VMEM((ROWS, wide), BF16)
    products = 5 if backward else 3
    outs = pl.pallas_call(
        backward_kernel if backward else forward_kernel,
        grid_spec=pltpu.PrefetchScalarGridSpec(
            num_scalar_prefetch=1,
            grid=(2,),
            in_specs=in_specs,
            out_specs=out_specs,
            scratch_shapes=[laid, laid, narrow, narrow] if backward else [laid, narrow],
        ),
        out_shape=out_shape,
        compiler_params=params(44 if backward else 34),
        cost_estimate=cost(
            2 * products * 2 * ROWS * 8 * HALF * wide, 30 * 2**20, 2 * ROWS * wide
        ),
    )(where, *near, *last, *rows, *weights)
    return outs[:4], outs[4:]


def weight_columns(idents, weights):
    experts = jnp.arange(32, dtype=jnp.int32)
    table = jnp.sum(
        jnp.where(idents[:, :, None] == experts[None, None, :], weights[:, :, None], 0.0), axis=1
    )
    high = lax.reduce_precision(table, exponent_bits=8, mantissa_bits=7)
    return [high.astype(BF16), (table - high).astype(BF16)]


def on_device(x_a, ids_a, prob_a, x_b, ids_b, prob_b, cot_b, w_gate, w_up, w_down):
    here = lax.axis_index("section").astype(jnp.int32)
    place = lax.axis_index("expert").astype(jnp.int32)
    core = here % 2
    group = jnp.where(core == 0, here // 2 % 4, here // 8)
    where = jnp.stack([place, here, here + 1 - 2 * core, group])
    meta = jnp.concatenate(weight_columns(ids_a, prob_a) + weight_columns(ids_b, prob_b), axis=1)
    inputs = (x_a, x_b, cot_b)
    def stack(parts):
        return jnp.concatenate(parts, axis=0)

    def together(*values):
        return lax.optimization_barrier(values)

    def gather_section(group):
        return lax.all_gather(
            group, "section", axis=0, tiled=True, axis_index_groups=LAST_GROUPS
        )

    def scatter_section(dense):
        return lax.psum_scatter(
            dense, "section", scatter_dimension=0, tiled=True, axis_index_groups=LAST_GROUPS
        )

    def cut(values):
        height = values.shape[0] // 4
        return [values[d * height : (d + 1) * height] for d in range(4)]

    def slot_rows(slots, dense):
        own, sibling = gather_last(where, slots, dense)
        return own, swap(sibling)

    quarters = spread(jnp.concatenate([v[:, HALF:] for v in inputs], axis=1), DEPTH)
    first = spread(jnp.concatenate([v[:, :HALF] for v in inputs] + [meta], axis=1), FIRST)
    quarters, first = together(quarters, first)

    whole_a = spread(stack([q[:, :HALF] for q in quarters]), FIRST)
    near = spread(stack(first), LAST)
    whole_a, near = together(whole_a, near)

    dense_a = gather_section(stack(whole_a))
    own, sibling, slots_a, slots_b = gather_first(where, near)
    whole_b = spread(stack([q[:, HALF:] for q in quarters]), FIRST)
    rows = (own, swap(sibling))
    near_a = spread(stack([r[:, NEAR_A : NEAR_A + HALF] for r in rows]), DEPTH)
    whole_b, near_a = together(whole_b, near_a)

    dense_b = gather_section(stack(whole_b))
    near_b = spread(stack([r[:, NEAR_B : NEAR_B + 2 * HALF] for r in rows]), DEPTH)
    last_a = slot_rows(slots_a, dense_a)
    near_a, (own, sibling) = expert_call(
        False, where, near_a, last_a, rows, w_gate, w_up, w_down
    )
    dense_a = scatter_last(where, slots_a, own, swap(sibling))
    near_b, dense_a = together(near_b, dense_a)

    group_a = scatter_section(dense_a)
    returned_a = collect(near_a, DEPTH)
    last_b = slot_rows(slots_b, dense_b)
    near_b, (own, sibling) = expert_call(True, where, near_b, last_b, rows, w_gate, w_up, w_down)
    dense_b = scatter_last(where, slots_b, own, swap(sibling))
    dense_b, returned_a = together(dense_b, returned_a)

    group_b = scatter_section(dense_b)
    returned_b = collect(near_b, DEPTH)
    parts_a = scatter_first(slots_a, returned_a[:ROWS], swap(returned_a[ROWS:]))
    first_a = collect(cut(collect(parts_a, LAST)), FIRST)
    last_a = collect(cut(collect(cut(group_a), FIRST)), DEPTH)
    first_a, last_a, returned_b = together(first_a, last_a, returned_b)

    parts_b = scatter_first(slots_b, returned_b[:ROWS], swap(returned_b[ROWS:]))
    group_b, parts_b = collect(cut(group_b), FIRST), collect(parts_b, LAST)
    last_b, first_b = collect(cut(group_b), DEPTH), collect(cut(parts_b), FIRST)
    return (
        jnp.concatenate([first_a, last_a], axis=1),
        jnp.concatenate([first_b, last_b], axis=1),
    )


def solution(mesh):
    in_specs = (
        P("section", "expert"),
        P("section", None),
        P("section", None),
        P("section", "expert"),
        P("section", None),
        P("section", None),
        P("section", "expert"),
        P("section", None, "expert"),
        P("section", None, "expert"),
        P("section", "expert", None),
    )
    out_specs = (P("section", "expert"), P("section", "expert"))
    return jax.shard_map(
        on_device, mesh=mesh, in_specs=in_specs, out_specs=out_specs, check_vma=False
    )
```

```python
import functools

import jax
import jax.numpy as jnp
from jax import lax
from jax.experimental import pallas as pl
from jax.experimental.pallas import tpu as pltpu
from jax.sharding import PartitionSpec as P

TOK = 64
CAP = 20
HALF = 512
CORES = 2
ROWS = 16 * CAP
GROUP = 4 * TOK
SLOTS = 4 * CAP
META = 128
BASES = (0, 64)
NEAR_A = 0
META_A = HALF
NEAR_B = HALF + META
META_B = 3 * HALF + META
BF16 = jnp.bfloat16
F32 = jnp.float32


def _section_moves(move):
    pairs = []
    for y in range(4):
        for x in range(4):
            for core in range(CORES):
                axis, shift = move[core]
                there_y = (y + shift) % 4 if axis == "y" else y
                there_x = (x + shift) % 4 if axis == "x" else x
                there_core = 1 - core if axis == "core" else core
                pairs.append(((y * 4 + x) * 2 + core, (there_y * 4 + there_x) * 2 + there_core))
    return pairs


def _shifts(axes):
    return [None] + [_section_moves(tuple((a, s) for a in axes)) for s in (1, 2, 3)]


def _groups(axes):
    groups = []
    for core in range(CORES):
        for other in range(4):
            if axes[core] == "y":
                groups.append([(i * 4 + other) * 2 + core for i in range(4)])
            else:
                groups.append([(other * 4 + i) * 2 + core for i in range(4)])
    return groups


FIRST = ("section", _shifts("yx"))
LAST = ("section", _shifts("xy"))
DEPTH = ("expert", [None] + [[(i, (i + s) % 4) for i in range(4)] for s in (1, 2, 3)])
LAST_GROUPS = _groups("xy")
SWAP = _section_moves((("core", 0), ("core", 0)))


def spread(values, ring):
    axis, shifts = ring
    return [values] + [lax.ppermute(values, axis, shifts[4 - d]) for d in (1, 2, 3)]


DEPTH_RING = [
    (s * 4 + z, s * 4 + (z + (1 if s % CORES == 0 else 3)) % 4) for s in range(32) for z in range(4)
]


def around(values, steps):
    parts = [values]
    for _ in range(steps):
        parts.append(lax.ppermute(parts[-1], ("section", "expert"), DEPTH_RING))
    return parts


def send(parts, ring):
    axis, shifts = ring
    return [parts[0]] + [lax.ppermute(parts[d], axis, shifts[d]) for d in (1, 2, 3)]


def total(parts):
    value = parts[0].astype(F32)
    for part in parts[1:]:
        value = value + part.astype(F32)
    return value.astype(BF16)


def swap(values):
    return lax.ppermute(values, "section", SWAP)


def dot(a, b):
    return jnp.dot(a, b, preferred_element_type=F32)


def dot_last(a, b):
    return lax.dot_general(a, b, (((1,), (1,)), ((), ())), preferred_element_type=F32)


def dot_first(a, b):
    return lax.dot_general(a, b, (((0,), (0,)), ((), ())), preferred_element_type=F32)


def params(mib):
    return pltpu.CompilerParams(vmem_limit_bytes=mib * 2**20)


def cost(flops, moved, transcendentals=0):
    return pl.CostEstimate(flops=flops // 64, bytes_accessed=moved // 64, transcendentals=0)


def slot_matrices(meta, here, sibling):
    rows = lax.broadcasted_iota(jnp.int32, (8, META), 0)
    lanes = lax.broadcasted_iota(jnp.int32, (8, META), 1)
    expert = jnp.where(rows % 2 == 0, here, sibling)
    wanted = jnp.where(rows < 2, BASES[0] + expert, jnp.where(rows < 4, BASES[1] + expert, -1))
    select = (lanes == wanted).astype(F32).astype(BF16)
    routed = (meta.astype(F32) > 0.0).astype(F32).astype(BF16)
    match = dot_last(select, routed)
    before = lax.broadcasted_iota(jnp.int32, (GROUP, GROUP), 0)
    token = lax.broadcasted_iota(jnp.int32, (GROUP, GROUP), 1)
    same = jnp.logical_and(before < token, before // TOK == token // TOK)
    rank = dot(match.astype(BF16), same.astype(F32).astype(BF16))
    block = lax.broadcasted_iota(jnp.int32, (8, GROUP), 1) // TOK
    place = jnp.where(match > 0.5, block * CAP + rank.astype(jnp.int32), -1)
    slot = lax.broadcasted_iota(jnp.int32, (SLOTS, GROUP), 0)
    pieces = [(slot == place[i : i + 1, :]).astype(F32) for i in range(4)]
    return [jnp.concatenate(pieces[i : i + 2], axis=0).astype(BF16) for i in (0, 2)]


def gather_first_kernel(where, *refs):
    parts, (own_ref, sibling_ref, ahead_ref, back_ref) = refs[:4], refs[4:]
    for group in range(4):
        values = parts[group][...]
        meta = values[:, 3 * HALF :]
        ahead, back = slot_matrices(meta, where[1], where[2])
        ahead_ref[group] = ahead
        back_ref[group] = back
        place = slice(group * SLOTS, (group + 1) * SLOTS)
        for slots, begin, end, column in (
            (ahead, 0, HALF, NEAR_A),
            (ahead, 3 * HALF, 3 * HALF + META, META_A),
            (back, HALF, 3 * HALF, NEAR_B),
            (back, 3 * HALF, 3 * HALF + META, META_B),
        ):
            picked = dot(slots, values[:, begin:end]).astype(BF16)
            own_ref[place, column : column + end - begin] = picked[:SLOTS]
            sibling_ref[place, column : column + end - begin] = picked[SLOTS:]


def gather_first(where, parts):
    width = 3 * HALF + 2 * META
    rows = jax.ShapeDtypeStruct((ROWS, width), BF16)
    slots = jax.ShapeDtypeStruct((4, 2 * SLOTS, GROUP), BF16)
    whole = pl.BlockSpec(memory_space=pltpu.VMEM)
    return pl.pallas_call(
        gather_first_kernel,
        in_specs=[pl.BlockSpec(memory_space=pltpu.SMEM)] + [whole] * 4,
        out_specs=[whole] * 4,
        out_shape=[rows, rows, slots, slots],
        compiler_params=params(16),
        cost_estimate=cost(2 * 4 * 2 * SLOTS * GROUP * width, 6 * 2**20),
    )(where, *parts)


def along(where, distance, width, size=HALF):
    start = lax.rem(where[0] + distance, 4) * width
    return pl.ds(pl.multiple_of(start, HALF), size)


def turned(where, number, width):
    start = lax.rem(where[0] + number * where[4], 4) * width
    return pl.ds(pl.multiple_of(start, HALF), HALF)


def gather_last_kernel(where, slots_ref, values_ref, own_ref, sibling_ref):
    for z in range(4):
        values = jnp.concatenate(
            [values_ref[pl.ds((4 * part + z) * TOK, TOK), :] for part in range(4)], axis=0
        )
        picked = dot(slots_ref[0], values).astype(BF16)
        columns = along(where, z, HALF)
        own_ref[:, columns] = picked[:SLOTS]
        sibling_ref[:, columns] = picked[SLOTS:]


def gather_last(where, slots, values):
    tensors = values.shape[1] // HALF
    shape = jax.ShapeDtypeStruct((ROWS, tensors * 4 * HALF), BF16)
    return pl.pallas_call(
        gather_last_kernel,
        grid_spec=pltpu.PrefetchScalarGridSpec(
            num_scalar_prefetch=1,
            grid=(tensors, 4),
            in_specs=[
                pl.BlockSpec((1, 2 * SLOTS, GROUP), lambda t, i, w: (i, 0, 0)),
                pl.BlockSpec((4 * GROUP, HALF), lambda t, i, w: (lax.rem(w[3] + i, 4), t)),
            ],
            out_specs=[pl.BlockSpec((SLOTS, 4 * HALF), lambda t, i, w: (i, t))] * 2,
        ),
        out_shape=[shape, shape],
        compiler_params=params(16),
        cost_estimate=cost(
            2 * 16 * 2 * SLOTS * GROUP * HALF * tensors, 14 * 2**20 * tensors
        ),
    )(where, slots, values)


def scatter_first_kernel(slots_ref, own_ref, sibling_ref, *outs):
    for group in range(4):
        place = slice(group * SLOTS, (group + 1) * SLOTS)
        rows = jnp.concatenate([own_ref[place, :], sibling_ref[place, :]], axis=0)
        outs[group][...] = dot_first(slots_ref[group], rows).astype(BF16)


def scatter_first(slots, own, sibling):
    whole = pl.BlockSpec(memory_space=pltpu.VMEM)
    return pl.pallas_call(
        scatter_first_kernel,
        in_specs=[whole] * 3,
        out_specs=[whole] * 4,
        out_shape=[jax.ShapeDtypeStruct((GROUP, HALF), BF16)] * 4,
        compiler_params=params(16),
        cost_estimate=cost(2 * 4 * 2 * SLOTS * GROUP * HALF, 3 * 2**20),
    )(slots, own, sibling)


def scatter_last_kernel(where, slots_ref, own_ref, sibling_ref, out_ref):
    for z in range(4):
        width = out_ref.shape[1]
        columns = along(where, z, width, width)
        rows = jnp.concatenate([own_ref[:, columns], sibling_ref[:, columns]], axis=0)
        dense = dot_first(slots_ref[0], rows).astype(BF16)
        for part in range(4):
            out_ref[pl.ds((4 * part + z) * TOK, TOK), :] = dense[part * TOK : (part + 1) * TOK]


def scatter_last(where, slots, own, sibling):
    width = own.shape[1] // 4
    return pl.pallas_call(
        scatter_last_kernel,
        grid_spec=pltpu.PrefetchScalarGridSpec(
            num_scalar_prefetch=1,
            grid=(4,),
            in_specs=[pl.BlockSpec((1, 2 * SLOTS, GROUP), lambda i, w: (i, 0, 0))]
            + [pl.BlockSpec((SLOTS, 4 * width), lambda i, w: (i, 0))] * 2,
            out_specs=pl.BlockSpec((4 * GROUP, width), lambda i, w: (lax.rem(w[3] + i, 4), 0)),
        ),
        out_shape=jax.ShapeDtypeStruct((16 * GROUP, width), BF16),
        compiler_params=params(16),
        cost_estimate=cost(2 * 16 * 2 * SLOTS * GROUP * width, 28 * 2**20),
    )(where, slots, own, sibling)


def feature_copies(where, near, last, target, sems, part, first_near, first_last, spot):
    copies = []
    for z in range(4):
        copies.append(
            pltpu.make_async_copy(
                near[z].at[pl.ds(part * ROWS, ROWS), pl.ds(first_near, HALF)],
                target.at[part, :, spot(where, z, 2 * HALF)],
                sems.at[part, 2 * z],
            )
        )
        copies.append(
            pltpu.make_async_copy(
                last[part].at[:, pl.ds(first_last + z * HALF, HALF)],
                target.at[part, :, pl.ds((2 * z + 1) * HALF, HALF)],
                sems.at[part, 2 * z + 1],
            )
        )
    return copies


def wait_part(copies):
    for part in range(2):

        @pl.when(pl.program_id(0) == part)
        def _():
            for copy in copies[part]:
                copy.wait()


def wait_first(copy):
    @pl.when(pl.program_id(0) == 0)
    def _():
        copy.wait()


def start_first(copies):
    @pl.when(pl.program_id(0) == 0)
    def _():
        for copy in copies:
            copy.start()


def write_result(weight, product, outs):
    for block in range(8):
        columns = slice(block * HALF, (block + 1) * HALF)
        value = (product(columns) * weight).astype(BF16)
        for part in range(2):

            @pl.when(pl.program_id(0) == part)
            def _():
                outs[part][:, columns] = value


def write_halves(where, weight, product, near, last):
    for z in range(4):
        near[z][...] = (product(along(where, z, 2 * HALF)) * weight).astype(BF16)
    for z in range(4):
        value = (product(pl.ds((2 * z + 1) * HALF, HALF)) * weight).astype(BF16)
        for part in range(2):

            @pl.when(pl.program_id(0) == part)
            def _():
                last[part][:, z * HALF : (z + 1) * HALF] = value


def pick(refs):
    return jnp.where(pl.program_id(0) == 0, refs[0][...], refs[1][...])


def slot_weight(rows, base, expert):
    lanes = lax.broadcasted_iota(jnp.int32, (ROWS, META), 1)
    chosen = jnp.logical_or(lanes == base + expert, lanes == base + 32 + expert)
    return jnp.sum(jnp.where(chosen, rows.astype(F32), 0.0), axis=1, keepdims=True)


def forward_kernel(where, *refs):
    near, last, metas, weights = refs[:4], refs[4:6], refs[6:8], refs[8:11]
    outs = refs[11:13]
    gate_ref, up_ref, down_ref, weight_sems, values, sems, hidden = refs[13:]
    step = pl.program_id(0)
    rows = [feature_copies(where, near, last, values, sems, p, 0, 0, along) for p in range(2)]
    held = (gate_ref, up_ref, down_ref)
    matrices = [pltpu.make_async_copy(weights[n], held[n], weight_sems.at[n]) for n in range(3)]
    start_first(rows[0] + matrices + rows[1])
    weight = slot_weight(pick(metas), BASES[0], where[1])
    wait_part(rows)
    wait_first(matrices[0])
    gate = dot(values[step], gate_ref[0])
    wait_first(matrices[1])
    upward = dot(values[step], up_ref[0])
    hidden[...] = (gate / (1.0 + jnp.exp(-gate)) * upward).astype(BF16)
    wait_first(matrices[2])

    def product(columns):
        return dot(hidden[...], down_ref[0, :, columns])

    write_result(weight, product, outs)


def backward_kernel(where, *refs):
    near, last, metas, weights = refs[:4], refs[4:6], refs[6:8], refs[8:11]
    near_out, last_out = refs[11:15], refs[15:17]
    gate_ref, up_ref, down_ref, weight_sems, values, sems = refs[17:23]
    cotangent, cot_sems, gate_grad, up_grad = refs[23:]
    step = pl.program_id(0)
    rows = [feature_copies(where, near, last, values, sems, p, 0, 0, turned) for p in range(2)]
    cots = [
        feature_copies(where, near, last, cotangent, cot_sems, p, HALF, 4 * HALF, turned)
        for p in range(2)
    ]
    held = (gate_ref, up_ref, down_ref)
    matrices = [pltpu.make_async_copy(weights[n], held[n], weight_sems.at[n]) for n in range(3)]
    start_first(rows[0] + matrices[:2] + cots[0] + matrices[2:] + rows[1] + cots[1])
    weight = slot_weight(pick(metas), BASES[1], where[1])
    wait_part(rows)
    wait_first(matrices[0])
    gate = dot(values[step], gate_ref[0])
    wait_first(matrices[1])
    upward = dot(values[step], up_ref[0])
    wait_part(cots)
    wait_first(matrices[2])
    grad = dot_last(cotangent[step], down_ref[0])
    sigmoid = 1.0 / (1.0 + jnp.exp(-gate))
    scaled = grad * sigmoid
    gate_grad[...] = (scaled * upward * (1.0 + gate * (1.0 - sigmoid))).astype(BF16)
    up_grad[...] = (scaled * gate).astype(BF16)

    def product(rows):
        return dot_last(gate_grad[...], gate_ref[0, rows]) + dot_last(up_grad[...], up_ref[0, rows])

    write_halves(where, weight, product, near_out, last_out)


def expert_call(backward, where, near, last, rows, w_gate, w_up, w_down):
    wide = w_gate.shape[2]
    column = (META_B if backward else META_A) // META
    once = pl.Buffered(1)
    anywhere = pl.BlockSpec(memory_space=pl.ANY)
    weights = [w_gate, w_up, w_down]
    in_specs = [anywhere] * 6
    in_specs += [
        pl.BlockSpec((ROWS, META), lambda i, w: (0, column), pipeline_mode=once) for _ in rows
    ]
    in_specs += [anywhere] * 3
    width = 4 * HALF if backward else 8 * HALF
    out_specs = [pl.BlockSpec((ROWS, HALF), lambda i, w: (i, 0))] * 4 if backward else []
    out_specs += [
        pl.BlockSpec((ROWS, width), lambda i, w: (0, 0), pipeline_mode=once) for _ in rows
    ]
    out_shape = [jax.ShapeDtypeStruct((2 * ROWS, HALF), BF16)] * 4 if backward else []
    out_shape += [jax.ShapeDtypeStruct((ROWS, width), BF16)] * 2
    laid = [pltpu.VMEM((2, ROWS, 8 * HALF), BF16), pltpu.SemaphoreType.DMA((2, 8))]
    narrow = pltpu.VMEM((ROWS, wide), BF16)
    scratch = [pltpu.VMEM(p.shape, BF16) for p in weights] + [pltpu.SemaphoreType.DMA((3,))]
    scratch += laid + laid + [narrow] * 2 if backward else laid + [narrow]
    products = 5 if backward else 3
    return pl.pallas_call(
        backward_kernel if backward else forward_kernel,
        grid_spec=pltpu.PrefetchScalarGridSpec(
            num_scalar_prefetch=1,
            grid=(2,),
            in_specs=in_specs,
            out_specs=out_specs,
            scratch_shapes=scratch,
        ),
        out_shape=out_shape,
        compiler_params=params(46 if backward else 40),
        cost_estimate=cost(
            2 * products * 2 * ROWS * 8 * HALF * wide, 30 * 2**20, 2 * ROWS * wide
        ),
    )(where, *near, *last, *rows, *weights)


def weight_columns(idents, weights):
    experts = jnp.arange(32, dtype=jnp.int32)
    table = jnp.sum(
        jnp.where(idents[:, :, None] == experts[None, None, :], weights[:, :, None], 0.0), axis=1
    )
    high = lax.reduce_precision(table, exponent_bits=8, mantissa_bits=7)
    return [high.astype(BF16), (table - high).astype(BF16)]


def on_device(x_a, ids_a, prob_a, x_b, ids_b, prob_b, cot_b, w_gate, w_up, w_down):
    here = lax.axis_index("section").astype(jnp.int32)
    place = lax.axis_index("expert").astype(jnp.int32)
    core = here % 2
    group = jnp.where(core == 0, here // 2 % 4, here // 8)
    where = jnp.stack([place, here, here + 1 - 2 * core, group, 3 - 2 * core])
    meta = jnp.concatenate(weight_columns(ids_a, prob_a) + weight_columns(ids_b, prob_b), axis=1)
    inputs = (x_a, x_b, cot_b)
    def stack(parts):
        return jnp.concatenate(parts, axis=0)

    def together(*values):
        return lax.optimization_barrier(values)

    def gather_section(group):
        return lax.all_gather(
            group, "section", axis=0, tiled=True, axis_index_groups=LAST_GROUPS
        )

    def scatter_section(dense):
        return lax.psum_scatter(
            dense, "section", scatter_dimension=0, tiled=True, axis_index_groups=LAST_GROUPS
        )

    def cut(values):
        height = values.shape[0] // 4
        return [values[d * height : (d + 1) * height] for d in range(4)]

    quarters = spread(jnp.concatenate([v[:, HALF:] for v in inputs], axis=1), DEPTH)
    first = spread(jnp.concatenate([v[:, :HALF] for v in inputs] + [meta], axis=1), FIRST)
    quarters, first = together(quarters, first)

    whole_a = spread(stack([q[:, :HALF] for q in quarters]), FIRST)
    near = spread(stack(first), LAST)
    whole_a, near = together(whole_a, near)

    dense_a = gather_section(stack(whole_a))
    own, sibling, slots_a, slots_b = gather_first(where, near)
    rows = (own, swap(sibling))
    near_a = spread(stack([r[:, NEAR_A : NEAR_A + HALF] for r in rows]), DEPTH)
    whole_b = spread(stack([q[:, HALF:] for q in quarters]), FIRST)
    whole_b, near_a, dense_a = together(whole_b, near_a, dense_a)

    dense_b = gather_section(stack(whole_b))
    own_a, sibling_a = gather_last(where, slots_a, dense_a)
    near_b = around(stack([r[:, NEAR_B : NEAR_B + 2 * HALF] for r in rows]), 1)
    near_b, sibling_a = together(near_b, swap(sibling_a))
    near_b += around(near_b[1], 1)[1:]
    own_a, sibling_a = expert_call(
        False, where, near_a, (own_a, sibling_a), rows, w_gate, w_up, w_down
    )
    near_b, own_a, sibling_a = together(near_b, own_a, sibling_a)
    near_b += around(near_b[2], 1)[1:]
    near_b, sibling_a, dense_b = together(near_b, swap(sibling_a), dense_b)

    group_a = scatter_section(scatter_last(where, slots_a, own_a, sibling_a))
    own, sibling = gather_last(where, slots_b, dense_b)
    sibling = swap(sibling)
    *near_b, own_b, sibling_b = expert_call(
        True, where, near_b, (own, sibling), rows, w_gate, w_up, w_down
    )
    own_b, sibling_b = together(own_b, swap(sibling_b))

    group_b = scatter_section(scatter_last(where, slots_b, own_b, sibling_b))
    near_b = send(near_b, DEPTH)
    group_a = send(cut(group_a), FIRST)
    near_b, group_a = together(near_b, group_a)

    returned_b = total(near_b)
    quarters_a = send(cut(total(group_a)), DEPTH)
    sibling_b, quarters_a, group_b = together(swap(returned_b[ROWS:]), quarters_a, group_b)

    parts_b = send(scatter_first(slots_b, returned_b[:ROWS], sibling_b), LAST)
    parts_b, group_b = together(parts_b, send(cut(group_b), FIRST))
    first_b, last_b = together(
        send(cut(total(parts_b)), FIRST), send(cut(total(group_b)), DEPTH)
    )
    return total(quarters_a), jnp.concatenate([total(first_b), total(last_b)], axis=1)


def solution(mesh):
    in_specs = (
        P("section", "expert"),
        P("section", None),
        P("section", None),
        P("section", "expert"),
        P("section", None),
        P("section", None),
        P("section", "expert"),
        P("section", None, "expert"),
        P("section", None, "expert"),
        P("section", "expert", None),
    )
    out_specs = (P("section", "expert"), P("section", "expert"))
    return jax.shard_map(
        on_device, mesh=mesh, in_specs=in_specs, out_specs=out_specs, check_vma=False
    )
```

```python
import functools

import jax
import jax.numpy as jnp
from jax import lax
from jax.experimental import pallas as pl
from jax.experimental.pallas import tpu as pltpu
from jax.sharding import PartitionSpec as P

TOK = 64
CAP = 20
HALF = 512
CORES = 2
ROWS = 16 * CAP
GROUP = 4 * TOK
SLOTS = 4 * CAP
META = 128
BASES = (0, 64)
NEAR_A = 0
META_A = HALF
NEAR_B = HALF + META
META_B = 3 * HALF + META
BF16 = jnp.bfloat16
F32 = jnp.float32


def _section_moves(move):
    pairs = []
    for y in range(4):
        for x in range(4):
            for core in range(CORES):
                axis, shift = move[core]
                there_y = (y + shift) % 4 if axis == "y" else y
                there_x = (x + shift) % 4 if axis == "x" else x
                there_core = 1 - core if axis == "core" else core
                pairs.append(((y * 4 + x) * 2 + core, (there_y * 4 + there_x) * 2 + there_core))
    return pairs


def _shifts(axes):
    return [None] + [_section_moves(tuple((a, s) for a in axes)) for s in (1, 2, 3)]


def _groups(axes):
    groups = []
    for core in range(CORES):
        for other in range(4):
            if axes[core] == "y":
                groups.append([(i * 4 + other) * 2 + core for i in range(4)])
            else:
                groups.append([(other * 4 + i) * 2 + core for i in range(4)])
    return groups


FIRST = ("section", _shifts("yx"))
LAST = ("section", _shifts("xy"))
DEPTH = ("expert", [None] + [[(i, (i + s) % 4) for i in range(4)] for s in (1, 2, 3)])
LAST_GROUPS = _groups("xy")
SWAP = _section_moves((("core", 0), ("core", 0)))


def spread(values, ring):
    axis, shifts = ring
    return [values] + [lax.ppermute(values, axis, shifts[4 - d]) for d in (1, 2, 3)]


DEPTH_RING = [
    (s * 4 + z, s * 4 + (z + (1 if s % CORES == 0 else 3)) % 4) for s in range(32) for z in range(4)
]


def around(values, steps):
    parts = [values]
    for _ in range(steps):
        parts.append(lax.ppermute(parts[-1], ("section", "expert"), DEPTH_RING))
    return parts


def send(parts, ring):
    axis, shifts = ring
    return [parts[0]] + [lax.ppermute(parts[d], axis, shifts[d]) for d in (1, 2, 3)]


def total(parts):
    value = parts[0].astype(F32)
    for part in parts[1:]:
        value = value + part.astype(F32)
    return value.astype(BF16)


def swap(values):
    return lax.ppermute(values, "section", SWAP)


def dot(a, b):
    return jnp.dot(a, b, preferred_element_type=F32)


def dot_last(a, b):
    return lax.dot_general(a, b, (((1,), (1,)), ((), ())), preferred_element_type=F32)


def dot_first(a, b):
    return lax.dot_general(a, b, (((0,), (0,)), ((), ())), preferred_element_type=F32)


def params(mib):
    return pltpu.CompilerParams(vmem_limit_bytes=mib * 2**20)


def cost(flops, moved, transcendentals=0):
    return pl.CostEstimate(flops=flops // 64, bytes_accessed=moved // 64, transcendentals=0)


def slot_matrices(meta, here, sibling):
    rows = lax.broadcasted_iota(jnp.int32, (8, META), 0)
    lanes = lax.broadcasted_iota(jnp.int32, (8, META), 1)
    expert = jnp.where(rows % 2 == 0, here, sibling)
    wanted = jnp.where(rows < 2, BASES[0] + expert, jnp.where(rows < 4, BASES[1] + expert, -1))
    select = (lanes == wanted).astype(F32).astype(BF16)
    routed = (meta.astype(F32) > 0.0).astype(F32).astype(BF16)
    match = dot_last(select, routed)
    before = lax.broadcasted_iota(jnp.int32, (GROUP, GROUP), 0)
    token = lax.broadcasted_iota(jnp.int32, (GROUP, GROUP), 1)
    same = jnp.logical_and(before < token, before // TOK == token // TOK)
    rank = dot(match.astype(BF16), same.astype(F32).astype(BF16))
    block = lax.broadcasted_iota(jnp.int32, (8, GROUP), 1) // TOK
    place = jnp.where(match > 0.5, block * CAP + rank.astype(jnp.int32), -1)
    slot = lax.broadcasted_iota(jnp.int32, (SLOTS, GROUP), 0)
    pieces = [(slot == place[i : i + 1, :]).astype(F32) for i in range(4)]
    return [jnp.concatenate(pieces[i : i + 2], axis=0).astype(BF16) for i in (0, 2)]


def gather_first_kernel(where, *refs):
    parts, (own_ref, sibling_ref, ahead_ref, back_ref) = refs[:4], refs[4:]
    for group in range(4):
        values = parts[group][...]
        meta = values[:, 3 * HALF :]
        ahead, back = slot_matrices(meta, where[1], where[2])
        ahead_ref[group] = ahead
        back_ref[group] = back
        place = slice(group * SLOTS, (group + 1) * SLOTS)
        for slots, begin, end, column in (
            (ahead, 0, HALF, NEAR_A),
            (ahead, 3 * HALF, 3 * HALF + META, META_A),
            (back, HALF, 3 * HALF, NEAR_B),
            (back, 3 * HALF, 3 * HALF + META, META_B),
        ):
            picked = dot(slots, values[:, begin:end]).astype(BF16)
            own_ref[place, column : column + end - begin] = picked[:SLOTS]
            sibling_ref[place, column : column + end - begin] = picked[SLOTS:]


def gather_first(where, parts):
    width = 3 * HALF + 2 * META
    rows = jax.ShapeDtypeStruct((ROWS, width), BF16)
    slots = jax.ShapeDtypeStruct((4, 2 * SLOTS, GROUP), BF16)
    whole = pl.BlockSpec(memory_space=pltpu.VMEM)
    return pl.pallas_call(
        gather_first_kernel,
        in_specs=[pl.BlockSpec(memory_space=pltpu.SMEM)] + [whole] * 4,
        out_specs=[whole] * 4,
        out_shape=[rows, rows, slots, slots],
        compiler_params=params(16),
        cost_estimate=cost(2 * 4 * 2 * SLOTS * GROUP * width, 6 * 2**20),
    )(where, *parts)


def along(where, distance, width, size=HALF):
    start = lax.rem(where[0] + distance, 4) * width
    return pl.ds(pl.multiple_of(start, HALF), size)


def turned(where, number, width):
    start = lax.rem(where[0] + number * where[4], 4) * width
    return pl.ds(pl.multiple_of(start, HALF), HALF)


def gather_last_kernel(where, slots_ref, values_ref, own_ref, sibling_ref):
    for z in range(4):
        values = jnp.concatenate(
            [values_ref[pl.ds((4 * part + z) * TOK, TOK), :] for part in range(4)], axis=0
        )
        picked = dot(slots_ref[0], values).astype(BF16)
        columns = along(where, z, HALF)
        own_ref[:, columns] = picked[:SLOTS]
        sibling_ref[:, columns] = picked[SLOTS:]


def gather_last(where, slots, values):
    tensors = values.shape[1] // HALF
    shape = jax.ShapeDtypeStruct((ROWS, tensors * 4 * HALF), BF16)
    return pl.pallas_call(
        gather_last_kernel,
        grid_spec=pltpu.PrefetchScalarGridSpec(
            num_scalar_prefetch=1,
            grid=(tensors, 4),
            in_specs=[
                pl.BlockSpec((1, 2 * SLOTS, GROUP), lambda t, i, w: (i, 0, 0)),
                pl.BlockSpec((4 * GROUP, HALF), lambda t, i, w: (lax.rem(w[3] + i, 4), t)),
            ],
            out_specs=[pl.BlockSpec((SLOTS, 4 * HALF), lambda t, i, w: (i, t))] * 2,
        ),
        out_shape=[shape, shape],
        compiler_params=params(16),
        cost_estimate=cost(
            2 * 16 * 2 * SLOTS * GROUP * HALF * tensors, 14 * 2**20 * tensors
        ),
    )(where, slots, values)


def scatter_first_kernel(slots_ref, own_ref, sibling_ref, *outs):
    for group in range(4):
        place = slice(group * SLOTS, (group + 1) * SLOTS)
        rows = jnp.concatenate([own_ref[place, :], sibling_ref[place, :]], axis=0)
        outs[group][...] = dot_first(slots_ref[group], rows).astype(BF16)


def scatter_first(slots, own, sibling):
    whole = pl.BlockSpec(memory_space=pltpu.VMEM)
    return pl.pallas_call(
        scatter_first_kernel,
        in_specs=[whole] * 3,
        out_specs=[whole] * 4,
        out_shape=[jax.ShapeDtypeStruct((GROUP, HALF), BF16)] * 4,
        compiler_params=params(16),
        cost_estimate=cost(2 * 4 * 2 * SLOTS * GROUP * HALF, 3 * 2**20),
    )(slots, own, sibling)


def scatter_last_kernel(where, slots_ref, own_ref, sibling_ref, out_ref):
    for z in range(4):
        width = out_ref.shape[1]
        columns = along(where, z, width, width)
        rows = jnp.concatenate([own_ref[:, columns], sibling_ref[:, columns]], axis=0)
        dense = dot_first(slots_ref[0], rows).astype(BF16)
        for part in range(4):
            out_ref[pl.ds((4 * part + z) * TOK, TOK), :] = dense[part * TOK : (part + 1) * TOK]


def scatter_last(where, slots, own, sibling):
    width = own.shape[1] // 4
    return pl.pallas_call(
        scatter_last_kernel,
        grid_spec=pltpu.PrefetchScalarGridSpec(
            num_scalar_prefetch=1,
            grid=(4,),
            in_specs=[pl.BlockSpec((1, 2 * SLOTS, GROUP), lambda i, w: (i, 0, 0))]
            + [pl.BlockSpec((SLOTS, 4 * width), lambda i, w: (i, 0))] * 2,
            out_specs=pl.BlockSpec((4 * GROUP, width), lambda i, w: (lax.rem(w[3] + i, 4), 0)),
        ),
        out_shape=jax.ShapeDtypeStruct((16 * GROUP, width), BF16),
        compiler_params=params(16),
        cost_estimate=cost(2 * 16 * 2 * SLOTS * GROUP * width, 28 * 2**20),
    )(where, slots, own, sibling)


def feature_copies(where, near, last, target, sems, part, first_near, first_last, spot):
    copies = []
    for z in range(4):
        copies.append(
            pltpu.make_async_copy(
                near[z].at[pl.ds(part * ROWS, ROWS), pl.ds(first_near, HALF)],
                target.at[part, :, spot(where, z, 2 * HALF)],
                sems.at[part, 2 * z],
            )
        )
        copies.append(
            pltpu.make_async_copy(
                last[part].at[:, pl.ds(first_last + z * HALF, HALF)],
                target.at[part, :, pl.ds((2 * z + 1) * HALF, HALF)],
                sems.at[part, 2 * z + 1],
            )
        )
    return copies


def wait_part(copies):
    for part in range(2):

        @pl.when(pl.program_id(0) == part)
        def _():
            for copy in copies[part]:
                copy.wait()


def wait_first(copy):
    @pl.when(pl.program_id(0) == 0)
    def _():
        copy.wait()


def start_first(copies):
    @pl.when(pl.program_id(0) == 0)
    def _():
        for copy in copies:
            copy.start()


def write_result(weight, product, outs):
    for block in range(8):
        columns = slice(block * HALF, (block + 1) * HALF)
        value = (product(columns) * weight).astype(BF16)
        for part in range(2):

            @pl.when(pl.program_id(0) == part)
            def _():
                outs[part][:, columns] = value


def write_halves(where, weight, product, near, last):
    for z in range(4):
        near[z][...] = (product(along(where, z, 2 * HALF)) * weight).astype(BF16)
    for z in range(4):
        value = (product(pl.ds((2 * z + 1) * HALF, HALF)) * weight).astype(BF16)
        for part in range(2):

            @pl.when(pl.program_id(0) == part)
            def _():
                last[part][:, z * HALF : (z + 1) * HALF] = value


def pick(refs):
    return jnp.where(pl.program_id(0) == 0, refs[0][...], refs[1][...])


def slot_weight(rows, base, expert):
    lanes = lax.broadcasted_iota(jnp.int32, (ROWS, META), 1)
    chosen = jnp.logical_or(lanes == base + expert, lanes == base + 32 + expert)
    return jnp.sum(jnp.where(chosen, rows.astype(F32), 0.0), axis=1, keepdims=True)


def forward_kernel(where, *refs):
    near, last, metas, weights = refs[:4], refs[4:6], refs[6:8], refs[8:11]
    outs = refs[11:13]
    gate_ref, up_ref, down_ref, weight_sems, values, sems, hidden = refs[13:]
    step = pl.program_id(0)
    rows = [feature_copies(where, near, last, values, sems, p, 0, 0, along) for p in range(2)]
    held = (gate_ref, up_ref, down_ref)
    matrices = [pltpu.make_async_copy(weights[n], held[n], weight_sems.at[n]) for n in range(3)]
    start_first(rows[0] + matrices + rows[1])
    weight = slot_weight(pick(metas), BASES[0], where[1])
    wait_part(rows)
    wait_first(matrices[0])
    gate = dot(values[step], gate_ref[0])
    wait_first(matrices[1])
    upward = dot(values[step], up_ref[0])
    hidden[...] = (gate / (1.0 + jnp.exp(-gate)) * upward).astype(BF16)
    wait_first(matrices[2])

    def product(columns):
        return dot(hidden[...], down_ref[0, :, columns])

    write_result(weight, product, outs)


def backward_kernel(where, *refs):
    near, last, metas, weights = refs[:4], refs[4:6], refs[6:8], refs[8:11]
    near_out, last_out = refs[11:15], refs[15:17]
    gate_ref, up_ref, down_ref, weight_sems, values, sems = refs[17:23]
    cotangent, cot_sems, gate_grad, up_grad = refs[23:]
    step = pl.program_id(0)
    rows = [feature_copies(where, near, last, values, sems, p, 0, 0, turned) for p in range(2)]
    cots = [
        feature_copies(where, near, last, cotangent, cot_sems, p, HALF, 4 * HALF, turned)
        for p in range(2)
    ]
    held = (gate_ref, up_ref, down_ref)
    matrices = [pltpu.make_async_copy(weights[n], held[n], weight_sems.at[n]) for n in range(3)]
    start_first(rows[0] + matrices[:2] + cots[0] + matrices[2:] + rows[1] + cots[1])
    weight = slot_weight(pick(metas), BASES[1], where[1])
    wait_part(rows)
    wait_first(matrices[0])
    gate = dot(values[step], gate_ref[0])
    wait_first(matrices[1])
    upward = dot(values[step], up_ref[0])
    wait_part(cots)
    wait_first(matrices[2])
    grad = dot_last(cotangent[step], down_ref[0])
    sigmoid = 1.0 / (1.0 + jnp.exp(-gate))
    scaled = grad * sigmoid
    gate_grad[...] = (scaled * upward * (1.0 + gate * (1.0 - sigmoid))).astype(BF16)
    up_grad[...] = (scaled * gate).astype(BF16)

    def product(rows):
        return dot_last(gate_grad[...], gate_ref[0, rows]) + dot_last(up_grad[...], up_ref[0, rows])

    write_halves(where, weight, product, near_out, last_out)


def expert_call(backward, where, near, last, rows, w_gate, w_up, w_down):
    wide = w_gate.shape[2]
    column = (META_B if backward else META_A) // META
    once = pl.Buffered(1)
    anywhere = pl.BlockSpec(memory_space=pl.ANY)
    weights = [w_gate, w_up, w_down]
    in_specs = [anywhere] * 6
    in_specs += [
        pl.BlockSpec((ROWS, META), lambda i, w: (0, column), pipeline_mode=once) for _ in rows
    ]
    in_specs += [anywhere] * 3
    width = 4 * HALF if backward else 8 * HALF
    out_specs = [pl.BlockSpec((ROWS, HALF), lambda i, w: (i, 0))] * 4 if backward else []
    out_specs += [
        pl.BlockSpec((ROWS, width), lambda i, w: (0, 0), pipeline_mode=once) for _ in rows
    ]
    out_shape = [jax.ShapeDtypeStruct((2 * ROWS, HALF), BF16)] * 4 if backward else []
    out_shape += [jax.ShapeDtypeStruct((ROWS, width), BF16)] * 2
    laid = [pltpu.VMEM((2, ROWS, 8 * HALF), BF16), pltpu.SemaphoreType.DMA((2, 8))]
    narrow = pltpu.VMEM((ROWS, wide), BF16)
    scratch = [pltpu.VMEM(p.shape, BF16) for p in weights] + [pltpu.SemaphoreType.DMA((3,))]
    scratch += laid + laid + [narrow] * 2 if backward else laid + [narrow]
    products = 5 if backward else 3
    return pl.pallas_call(
        backward_kernel if backward else forward_kernel,
        grid_spec=pltpu.PrefetchScalarGridSpec(
            num_scalar_prefetch=1,
            grid=(2,),
            in_specs=in_specs,
            out_specs=out_specs,
            scratch_shapes=scratch,
        ),
        out_shape=out_shape,
        compiler_params=params(46 if backward else 40),
        cost_estimate=cost(
            2 * products * 2 * ROWS * 8 * HALF * wide, 30 * 2**20, 2 * ROWS * wide
        ),
    )(where, *near, *last, *rows, *weights)


def weight_columns(idents, weights):
    experts = jnp.arange(32, dtype=jnp.int32)
    table = jnp.sum(
        jnp.where(idents[:, :, None] == experts[None, None, :], weights[:, :, None], 0.0), axis=1
    )
    high = lax.reduce_precision(table, exponent_bits=8, mantissa_bits=7)
    return [high.astype(BF16), (table - high).astype(BF16)]


def on_device(x_a, ids_a, prob_a, x_b, ids_b, prob_b, cot_b, w_gate, w_up, w_down):
    here = lax.axis_index("section").astype(jnp.int32)
    place = lax.axis_index("expert").astype(jnp.int32)
    core = here % 2
    group = jnp.where(core == 0, here // 2 % 4, here // 8)
    where = jnp.stack([place, here, here + 1 - 2 * core, group, 3 - 2 * core])
    meta = jnp.concatenate(weight_columns(ids_a, prob_a) + weight_columns(ids_b, prob_b), axis=1)
    inputs = (x_a, x_b, cot_b)
    def stack(parts):
        return jnp.concatenate(parts, axis=0)

    def together(*values):
        return lax.optimization_barrier(values)

    def gather_section(group):
        return lax.all_gather(
            group, "section", axis=0, tiled=True, axis_index_groups=LAST_GROUPS
        )

    def scatter_section(dense):
        return lax.psum_scatter(
            dense, "section", scatter_dimension=0, tiled=True, axis_index_groups=LAST_GROUPS
        )

    def cut(values):
        height = values.shape[0] // 4
        return [values[d * height : (d + 1) * height] for d in range(4)]

    quarters = spread(jnp.concatenate([v[:, HALF:] for v in inputs], axis=1), DEPTH)
    first = spread(jnp.concatenate([v[:, :HALF] for v in inputs] + [meta], axis=1), FIRST)
    quarters, first = together(quarters, first)

    whole_a = spread(stack([q[:, :HALF] for q in quarters]), FIRST)
    near = spread(stack(first), LAST)
    whole_a, near = together(whole_a, near)

    dense_a = gather_section(stack(whole_a))
    own, sibling, slots_a, slots_b = gather_first(where, near)
    rows = (own, swap(sibling))
    near_a = spread(stack([r[:, NEAR_A : NEAR_A + HALF] for r in rows]), DEPTH)
    whole_b = spread(stack([q[:, HALF:] for q in quarters]), FIRST)
    whole_b, near_a, dense_a = together(whole_b, near_a, dense_a)

    dense_b = gather_section(stack(whole_b))
    own_a, sibling_a = gather_last(where, slots_a, dense_a)
    near_b = around(stack([r[:, NEAR_B : NEAR_B + 2 * HALF] for r in rows]), 1)
    near_b, sibling_a = together(near_b, swap(sibling_a))
    near_b += around(near_b[1], 1)[1:]
    own_a, sibling_a = expert_call(
        False, where, near_a, (own_a, sibling_a), rows, w_gate, w_up, w_down
    )
    near_b, own_a, sibling_a = together(near_b, own_a, sibling_a)
    near_b += around(near_b[2], 1)[1:]
    near_b, sibling_a, dense_b = together(near_b, swap(sibling_a), dense_b)

    group_a = scatter_section(scatter_last(where, slots_a, own_a, sibling_a))
    own, sibling = gather_last(where, slots_b, dense_b)
    sibling = swap(sibling)
    *near_b, own_b, sibling_b = expert_call(
        True, where, near_b, (own, sibling), rows, w_gate, w_up, w_down
    )
    own_b, sibling_b = together(own_b, swap(sibling_b))

    group_b = scatter_section(scatter_last(where, slots_b, own_b, sibling_b))
    near_b = together(*send(near_b, DEPTH))

    returned_b = total(near_b)
    sibling_b, group_a, group_b = together(swap(returned_b[ROWS:]), group_a, group_b)

    parts_b = send(scatter_first(slots_b, returned_b[:ROWS], sibling_b), LAST)
    pairs = zip(cut(group_a), cut(group_b))
    whole = send([jnp.concatenate(pair, axis=1) for pair in pairs], FIRST)
    parts_b, whole = together(parts_b, whole)

    first_b, last = together(send(cut(total(parts_b)), FIRST), send(cut(total(whole)), DEPTH))
    last = total(last)
    return last[:, : 2 * HALF], jnp.concatenate([total(first_b), last[:, 2 * HALF :]], axis=1)


def solution(mesh):
    in_specs = (
        P("section", "expert"),
        P("section", None),
        P("section", None),
        P("section", "expert"),
        P("section", None),
        P("section", None),
        P("section", "expert"),
        P("section", None, "expert"),
        P("section", None, "expert"),
        P("section", "expert", None),
    )
    out_specs = (P("section", "expert"), P("section", "expert"))
    return jax.shard_map(
        on_device, mesh=mesh, in_specs=in_specs, out_specs=out_specs, check_vma=False
    )
```

```python
import functools

import jax
import jax.numpy as jnp
from jax import lax
from jax.experimental import pallas as pl
from jax.experimental.pallas import tpu as pltpu
from jax.sharding import PartitionSpec as P

TOK = 64
CAP = 20
HALF = 512
CORES = 2
ROWS = 16 * CAP
GROUP = 4 * TOK
SLOTS = 4 * CAP
META = 128
BASES = (0, 64)
NEAR_A = 0
META_A = HALF
NEAR_B = HALF + META
META_B = 3 * HALF + META
BF16 = jnp.bfloat16
F32 = jnp.float32


def _section_moves(move):
    pairs = []
    for y in range(4):
        for x in range(4):
            for core in range(CORES):
                axis, shift = move[core]
                there_y = (y + shift) % 4 if axis == "y" else y
                there_x = (x + shift) % 4 if axis == "x" else x
                there_core = 1 - core if axis == "core" else core
                pairs.append(((y * 4 + x) * 2 + core, (there_y * 4 + there_x) * 2 + there_core))
    return pairs


def _shifts(axes):
    return [None] + [_section_moves(tuple((a, s) for a in axes)) for s in (1, 2, 3)]


def _groups(axes):
    groups = []
    for core in range(CORES):
        for other in range(4):
            if axes[core] == "y":
                groups.append([(i * 4 + other) * 2 + core for i in range(4)])
            else:
                groups.append([(other * 4 + i) * 2 + core for i in range(4)])
    return groups


FIRST = ("section", _shifts("yx"))
LAST = ("section", _shifts("xy"))
DEPTH = ("expert", [None] + [[(i, (i + s) % 4) for i in range(4)] for s in (1, 2, 3)])
LAST_GROUPS = _groups("xy")
SWAP = _section_moves((("core", 0), ("core", 0)))


def spread(values, ring):
    axis, shifts = ring
    return [values] + [lax.ppermute(values, axis, shifts[4 - d]) for d in (1, 2, 3)]


DEPTH_RING = [
    (s * 4 + z, s * 4 + (z + (1 if s % CORES == 0 else 3)) % 4) for s in range(32) for z in range(4)
]


def around(values, steps):
    parts = [values]
    for _ in range(steps):
        parts.append(lax.ppermute(parts[-1], ("section", "expert"), DEPTH_RING))
    return parts


def send(parts, ring):
    axis, shifts = ring
    return [parts[0]] + [lax.ppermute(parts[d], axis, shifts[d]) for d in (1, 2, 3)]


def total(parts):
    value = parts[0].astype(F32)
    for part in parts[1:]:
        value = value + part.astype(F32)
    return value.astype(BF16)


def swap(values):
    return lax.ppermute(values, "section", SWAP)


def dot(a, b):
    return jnp.dot(a, b, preferred_element_type=F32)


def dot_last(a, b):
    return lax.dot_general(a, b, (((1,), (1,)), ((), ())), preferred_element_type=F32)


def dot_first(a, b):
    return lax.dot_general(a, b, (((0,), (0,)), ((), ())), preferred_element_type=F32)


def params(mib):
    return pltpu.CompilerParams(vmem_limit_bytes=mib * 2**20)


def cost(flops, moved, transcendentals=0):
    return pl.CostEstimate(flops=flops // 64, bytes_accessed=moved // 64, transcendentals=0)


def slot_matrices(meta, here, sibling):
    rows = lax.broadcasted_iota(jnp.int32, (8, META), 0)
    lanes = lax.broadcasted_iota(jnp.int32, (8, META), 1)
    expert = jnp.where(rows % 2 == 0, here, sibling)
    wanted = jnp.where(rows < 2, BASES[0] + expert, jnp.where(rows < 4, BASES[1] + expert, -1))
    select = (lanes == wanted).astype(F32).astype(BF16)
    routed = (meta.astype(F32) > 0.0).astype(F32).astype(BF16)
    match = dot_last(select, routed)
    before = lax.broadcasted_iota(jnp.int32, (GROUP, GROUP), 0)
    token = lax.broadcasted_iota(jnp.int32, (GROUP, GROUP), 1)
    same = jnp.logical_and(before < token, before // TOK == token // TOK)
    rank = dot(match.astype(BF16), same.astype(F32).astype(BF16))
    block = lax.broadcasted_iota(jnp.int32, (8, GROUP), 1) // TOK
    place = jnp.where(match > 0.5, block * CAP + rank.astype(jnp.int32), -1)
    slot = lax.broadcasted_iota(jnp.int32, (SLOTS, GROUP), 0)
    pieces = [(slot == place[i : i + 1, :]).astype(F32) for i in range(4)]
    return [jnp.concatenate(pieces[i : i + 2], axis=0).astype(BF16) for i in (0, 2)]


def gather_first_kernel(where, *refs):
    parts, (own_ref, sibling_ref, ahead_ref, back_ref) = refs[:4], refs[4:]
    for group in range(4):
        values = parts[group][...]
        meta = values[:, 3 * HALF :]
        ahead, back = slot_matrices(meta, where[1], where[2])
        ahead_ref[group] = ahead
        back_ref[group] = back
        place = slice(group * SLOTS, (group + 1) * SLOTS)
        for slots, begin, end, column in (
            (ahead, 0, HALF, NEAR_A),
            (ahead, 3 * HALF, 3 * HALF + META, META_A),
            (back, HALF, 3 * HALF, NEAR_B),
            (back, 3 * HALF, 3 * HALF + META, META_B),
        ):
            picked = dot(slots, values[:, begin:end]).astype(BF16)
            own_ref[place, column : column + end - begin] = picked[:SLOTS]
            sibling_ref[place, column : column + end - begin] = picked[SLOTS:]


def gather_first(where, parts):
    width = 3 * HALF + 2 * META
    rows = jax.ShapeDtypeStruct((ROWS, width), BF16)
    slots = jax.ShapeDtypeStruct((4, 2 * SLOTS, GROUP), BF16)
    whole = pl.BlockSpec(memory_space=pltpu.VMEM)
    return pl.pallas_call(
        gather_first_kernel,
        in_specs=[pl.BlockSpec(memory_space=pltpu.SMEM)] + [whole] * 4,
        out_specs=[whole] * 4,
        out_shape=[rows, rows, slots, slots],
        compiler_params=params(16),
        cost_estimate=cost(2 * 4 * 2 * SLOTS * GROUP * width, 6 * 2**20),
    )(where, *parts)


def along(where, distance, width, size=HALF):
    start = lax.rem(where[0] + distance, 4) * width
    return pl.ds(pl.multiple_of(start, HALF), size)


def turned(where, number, width):
    start = lax.rem(where[0] + number * where[4], 4) * width
    return pl.ds(pl.multiple_of(start, HALF), HALF)


def gather_last_kernel(where, slots_ref, values_ref, own_ref, sibling_ref):
    for z in range(4):
        values = jnp.concatenate(
            [values_ref[pl.ds((4 * part + z) * TOK, TOK), :] for part in range(4)], axis=0
        )
        picked = dot(slots_ref[0], values).astype(BF16)
        columns = along(where, z, HALF)
        own_ref[:, columns] = picked[:SLOTS]
        sibling_ref[:, columns] = picked[SLOTS:]


def gather_last(where, slots, values):
    tensors = values.shape[1] // HALF
    shape = jax.ShapeDtypeStruct((ROWS, tensors * 4 * HALF), BF16)
    return pl.pallas_call(
        gather_last_kernel,
        grid_spec=pltpu.PrefetchScalarGridSpec(
            num_scalar_prefetch=1,
            grid=(tensors, 4),
            in_specs=[
                pl.BlockSpec((1, 2 * SLOTS, GROUP), lambda t, i, w: (i, 0, 0)),
                pl.BlockSpec((4 * GROUP, HALF), lambda t, i, w: (lax.rem(w[3] + i, 4), t)),
            ],
            out_specs=[pl.BlockSpec((SLOTS, 4 * HALF), lambda t, i, w: (i, t))] * 2,
        ),
        out_shape=[shape, shape],
        compiler_params=params(16),
        cost_estimate=cost(
            2 * 16 * 2 * SLOTS * GROUP * HALF * tensors, 14 * 2**20 * tensors
        ),
    )(where, slots, values)


def scatter_first_kernel(slots_ref, own_ref, sibling_ref, *outs):
    for group in range(4):
        place = slice(group * SLOTS, (group + 1) * SLOTS)
        rows = jnp.concatenate([own_ref[place, :], sibling_ref[place, :]], axis=0)
        outs[group][...] = dot_first(slots_ref[group], rows).astype(BF16)


def scatter_first(slots, own, sibling):
    whole = pl.BlockSpec(memory_space=pltpu.VMEM)
    return pl.pallas_call(
        scatter_first_kernel,
        in_specs=[whole] * 3,
        out_specs=[whole] * 4,
        out_shape=[jax.ShapeDtypeStruct((GROUP, HALF), BF16)] * 4,
        compiler_params=params(16),
        cost_estimate=cost(2 * 4 * 2 * SLOTS * GROUP * HALF, 3 * 2**20),
    )(slots, own, sibling)


def scatter_last_kernel(where, slots_ref, own_ref, sibling_ref, out_ref):
    for z in range(4):
        width = out_ref.shape[1]
        columns = along(where, z, width, width)
        rows = jnp.concatenate([own_ref[:, columns], sibling_ref[:, columns]], axis=0)
        dense = dot_first(slots_ref[0], rows).astype(BF16)
        for part in range(4):
            out_ref[pl.ds((4 * part + z) * TOK, TOK), :] = dense[part * TOK : (part + 1) * TOK]


def scatter_last(where, slots, own, sibling):
    width = own.shape[1] // 4
    return pl.pallas_call(
        scatter_last_kernel,
        grid_spec=pltpu.PrefetchScalarGridSpec(
            num_scalar_prefetch=1,
            grid=(4,),
            in_specs=[pl.BlockSpec((1, 2 * SLOTS, GROUP), lambda i, w: (i, 0, 0))]
            + [pl.BlockSpec((SLOTS, 4 * width), lambda i, w: (i, 0))] * 2,
            out_specs=pl.BlockSpec((4 * GROUP, width), lambda i, w: (lax.rem(w[3] + i, 4), 0)),
        ),
        out_shape=jax.ShapeDtypeStruct((16 * GROUP, width), BF16),
        compiler_params=params(16),
        cost_estimate=cost(2 * 16 * 2 * SLOTS * GROUP * width, 28 * 2**20),
    )(where, slots, own, sibling)


def feature_copies(where, near, last, target, sems, part, first_near, first_last, spot):
    copies = []
    for z in range(4):
        copies.append(
            pltpu.make_async_copy(
                near[z].at[pl.ds(part * ROWS, ROWS), pl.ds(first_near, HALF)],
                target.at[part, :, spot(where, z, 2 * HALF)],
                sems.at[part, 2 * z],
            )
        )
        copies.append(
            pltpu.make_async_copy(
                last[part].at[:, pl.ds(first_last + z * HALF, HALF)],
                target.at[part, :, pl.ds((2 * z + 1) * HALF, HALF)],
                sems.at[part, 2 * z + 1],
            )
        )
    return copies


def wait_part(copies):
    for part in range(2):

        @pl.when(pl.program_id(0) == part)
        def _():
            for copy in copies[part]:
                copy.wait()


def wait_first(copy):
    @pl.when(pl.program_id(0) == 0)
    def _():
        copy.wait()


def start_first(copies):
    @pl.when(pl.program_id(0) == 0)
    def _():
        for copy in copies:
            copy.start()


def write_result(weight, product, outs):
    for block in range(8):
        columns = slice(block * HALF, (block + 1) * HALF)
        value = (product(columns) * weight).astype(BF16)
        for part in range(2):

            @pl.when(pl.program_id(0) == part)
            def _():
                outs[part][:, columns] = value


def write_halves(where, weight, product, near, last):
    for z in range(4):
        near[z][...] = (product(along(where, z, 2 * HALF)) * weight).astype(BF16)
    for z in range(4):
        value = (product(pl.ds((2 * z + 1) * HALF, HALF)) * weight).astype(BF16)
        for part in range(2):

            @pl.when(pl.program_id(0) == part)
            def _():
                last[part][:, z * HALF : (z + 1) * HALF] = value


def pick(refs):
    return jnp.where(pl.program_id(0) == 0, refs[0][...], refs[1][...])


def slot_weight(rows, base, expert):
    lanes = lax.broadcasted_iota(jnp.int32, (ROWS, META), 1)
    chosen = jnp.logical_or(lanes == base + expert, lanes == base + 32 + expert)
    return jnp.sum(jnp.where(chosen, rows.astype(F32), 0.0), axis=1, keepdims=True)


def forward_kernel(where, *refs):
    near, last, metas, weights = refs[:4], refs[4:6], refs[6:8], refs[8:11]
    outs = refs[11:13]
    gate_ref, up_ref, down_ref, weight_sems, values, sems, hidden = refs[13:]
    step = pl.program_id(0)
    rows = [feature_copies(where, near, last, values, sems, p, 0, 0, along) for p in range(2)]
    held = (gate_ref, up_ref, down_ref)
    matrices = [pltpu.make_async_copy(weights[n], held[n], weight_sems.at[n]) for n in range(3)]
    start_first(rows[0] + matrices + rows[1])
    weight = slot_weight(pick(metas), BASES[0], where[1])
    wait_part(rows)
    wait_first(matrices[0])
    gate = dot(values[step], gate_ref[0])
    wait_first(matrices[1])
    upward = dot(values[step], up_ref[0])
    hidden[...] = (gate / (1.0 + jnp.exp(-gate)) * upward).astype(BF16)
    wait_first(matrices[2])

    def product(columns):
        return dot(hidden[...], down_ref[0, :, columns])

    write_result(weight, product, outs)


def backward_kernel(where, *refs):
    near, last, metas, weights = refs[:4], refs[4:6], refs[6:8], refs[8:11]
    near_out, last_out = refs[11:15], refs[15:17]
    gate_ref, up_ref, down_ref, weight_sems, values, sems = refs[17:23]
    cotangent, cot_sems, gate_grad, up_grad = refs[23:]
    step = pl.program_id(0)
    rows = [feature_copies(where, near, last, values, sems, p, 0, 0, turned) for p in range(2)]
    cots = [
        feature_copies(where, near, last, cotangent, cot_sems, p, HALF, 4 * HALF, turned)
        for p in range(2)
    ]
    held = (gate_ref, up_ref, down_ref)
    matrices = [pltpu.make_async_copy(weights[n], held[n], weight_sems.at[n]) for n in range(3)]
    start_first(rows[0] + matrices[:2] + cots[0] + matrices[2:] + rows[1] + cots[1])
    weight = slot_weight(pick(metas), BASES[1], where[1])
    wait_part(rows)
    wait_first(matrices[0])
    gate = dot(values[step], gate_ref[0])
    wait_first(matrices[1])
    upward = dot(values[step], up_ref[0])
    wait_part(cots)
    wait_first(matrices[2])
    grad = dot_last(cotangent[step], down_ref[0])
    sigmoid = 1.0 / (1.0 + jnp.exp(-gate))
    scaled = grad * sigmoid
    gate_grad[...] = (scaled * upward * (1.0 + gate * (1.0 - sigmoid))).astype(BF16)
    up_grad[...] = (scaled * gate).astype(BF16)

    def product(rows):
        return dot_last(gate_grad[...], gate_ref[0, rows]) + dot_last(up_grad[...], up_ref[0, rows])

    write_halves(where, weight, product, near_out, last_out)


def expert_call(backward, where, near, last, rows, w_gate, w_up, w_down):
    wide = w_gate.shape[2]
    column = (META_B if backward else META_A) // META
    once = pl.Buffered(1)
    anywhere = pl.BlockSpec(memory_space=pl.ANY)
    weights = [w_gate, w_up, w_down]
    in_specs = [anywhere] * 6
    in_specs += [
        pl.BlockSpec((ROWS, META), lambda i, w: (0, column), pipeline_mode=once) for _ in rows
    ]
    in_specs += [anywhere] * 3
    width = 4 * HALF if backward else 8 * HALF
    out_specs = [pl.BlockSpec((ROWS, HALF), lambda i, w: (i, 0))] * 4 if backward else []
    out_specs += [
        pl.BlockSpec((ROWS, width), lambda i, w: (0, 0), pipeline_mode=once) for _ in rows
    ]
    out_shape = [jax.ShapeDtypeStruct((2 * ROWS, HALF), BF16)] * 4 if backward else []
    out_shape += [jax.ShapeDtypeStruct((ROWS, width), BF16)] * 2
    laid = [pltpu.VMEM((2, ROWS, 8 * HALF), BF16), pltpu.SemaphoreType.DMA((2, 8))]
    narrow = pltpu.VMEM((ROWS, wide), BF16)
    scratch = [pltpu.VMEM(p.shape, BF16) for p in weights] + [pltpu.SemaphoreType.DMA((3,))]
    scratch += laid + laid + [narrow] * 2 if backward else laid + [narrow]
    products = 5 if backward else 3
    return pl.pallas_call(
        backward_kernel if backward else forward_kernel,
        grid_spec=pltpu.PrefetchScalarGridSpec(
            num_scalar_prefetch=1,
            grid=(2,),
            in_specs=in_specs,
            out_specs=out_specs,
            scratch_shapes=scratch,
        ),
        out_shape=out_shape,
        compiler_params=params(46 if backward else 40),
        cost_estimate=cost(
            2 * products * 2 * ROWS * 8 * HALF * wide, 30 * 2**20, 2 * ROWS * wide
        ),
    )(where, *near, *last, *rows, *weights)


def weight_columns(idents, weights):
    experts = jnp.arange(32, dtype=jnp.int32)
    table = jnp.sum(
        jnp.where(idents[:, :, None] == experts[None, None, :], weights[:, :, None], 0.0), axis=1
    )
    high = lax.reduce_precision(table, exponent_bits=8, mantissa_bits=7)
    return [high.astype(BF16), (table - high).astype(BF16)]


def on_device(x_a, ids_a, prob_a, x_b, ids_b, prob_b, cot_b, w_gate, w_up, w_down):
    here = lax.axis_index("section").astype(jnp.int32)
    place = lax.axis_index("expert").astype(jnp.int32)
    core = here % 2
    group = jnp.where(core == 0, here // 2 % 4, here // 8)
    where = jnp.stack([place, here, here + 1 - 2 * core, group, 3 - 2 * core])
    meta = jnp.concatenate(weight_columns(ids_a, prob_a) + weight_columns(ids_b, prob_b), axis=1)
    inputs = (x_a, x_b, cot_b)
    def stack(parts):
        return jnp.concatenate(parts, axis=0)

    def together(*values):
        return lax.optimization_barrier(values)

    def gather_section(group):
        return lax.all_gather(
            group, "section", axis=0, tiled=True, axis_index_groups=LAST_GROUPS
        )

    def scatter_section(dense):
        return lax.psum_scatter(
            dense, "section", scatter_dimension=0, tiled=True, axis_index_groups=LAST_GROUPS
        )

    def cut(values):
        height = values.shape[0] // 4
        return [values[d * height : (d + 1) * height] for d in range(4)]

    quarters = spread(jnp.concatenate([v[:, HALF:] for v in inputs], axis=1), DEPTH)
    first = spread(jnp.concatenate([v[:, :HALF] for v in inputs] + [meta], axis=1), FIRST)
    quarters, first = together(quarters, first)

    whole_a = spread(stack([q[:, :HALF] for q in quarters]), FIRST)
    near = spread(stack(first), LAST)
    whole_a, near = together(whole_a, near)

    dense_a = gather_section(stack(whole_a))
    own, sibling, slots_a, slots_b = gather_first(where, near)
    rows = (own, swap(sibling))
    near_a = spread(stack([r[:, NEAR_A : NEAR_A + HALF] for r in rows]), DEPTH)
    whole_b = spread(stack([q[:, HALF:] for q in quarters]), FIRST)
    whole_b, near_a, dense_a = together(whole_b, near_a, dense_a)

    dense_b = gather_section(stack(whole_b))
    own_a, sibling_a = gather_last(where, slots_a, dense_a)
    near_b = around(stack([r[:, NEAR_B : NEAR_B + 2 * HALF] for r in rows]), 1)
    near_b, sibling_a = together(near_b, swap(sibling_a))
    near_b += around(near_b[1], 1)[1:]
    own_a, sibling_a = expert_call(
        False, where, near_a, (own_a, sibling_a), rows, w_gate, w_up, w_down
    )
    near_b, own_a, sibling_a = together(near_b, own_a, sibling_a)
    near_b += around(near_b[2], 1)[1:]
    near_b, sibling_a, dense_b = together(near_b, swap(sibling_a), dense_b)

    dense_a = scatter_last(where, slots_a, own_a, sibling_a)
    own, sibling = gather_last(where, slots_b, dense_b)
    sibling, dense_a = together(swap(sibling), dense_a)
    group_a = scatter_section(dense_a)
    *near_b, own_b, sibling_b = expert_call(
        True, where, near_b, (own, sibling), rows, w_gate, w_up, w_down
    )
    own_b, sibling_b = together(own_b, swap(sibling_b))

    group_b = scatter_section(scatter_last(where, slots_b, own_b, sibling_b))
    near_b = together(*send(near_b, DEPTH))

    returned_b = total(near_b)
    sibling_b, group_a, group_b = together(swap(returned_b[ROWS:]), group_a, group_b)

    parts_b = send(scatter_first(slots_b, returned_b[:ROWS], sibling_b), LAST)
    pairs = zip(cut(group_a), cut(group_b))
    whole = send([jnp.concatenate(pair, axis=1) for pair in pairs], FIRST)
    parts_b, whole = together(parts_b, whole)

    first_b, last = together(send(cut(total(parts_b)), FIRST), send(cut(total(whole)), DEPTH))
    last = total(last)
    return last[:, : 2 * HALF], jnp.concatenate([total(first_b), last[:, 2 * HALF :]], axis=1)


def solution(mesh):
    in_specs = (
        P("section", "expert"),
        P("section", None),
        P("section", None),
        P("section", "expert"),
        P("section", None),
        P("section", None),
        P("section", "expert"),
        P("section", None, "expert"),
        P("section", None, "expert"),
        P("section", "expert", None),
    )
    out_specs = (P("section", "expert"), P("section", "expert"))
    return jax.shard_map(
        on_device, mesh=mesh, in_specs=in_specs, out_specs=out_specs, check_vma=False
    )
```
